128 devices in a mesh: wide: 16 (over x, y_lo, core), narrow: 8 (over y_hi, z).
Axes of the slice: x: 4, y: 4 (y_hi: 2, y_lo: 2; y = y_hi * 2 + y_lo), z: 4, core: 2. Of those that a mesh axis runs over, the one named last changes fastest.
Arguments:
- object_field: float32 [2, 4096, 16384], P(None, 'narrow', 'wide'), may hold values from -6 to 6
- probe_modes: float32 [4, 2, 256, 256], replicated, may hold values from -4 to 4
- amplitudes: float32 [8, 16, 6, 256, 256], P('narrow', 'wide'), may hold values from 0.5 to 4
- offsets: int32 [2, 8, 16, 6], P(None, 'narrow', 'wide'), may hold values from 0 to 1024, as said below
- counts: int32 [8, 16], P('narrow', 'wide'), may hold values from 1 to 6, as said below
Outputs:
- new_object: float32 [2, 4096, 16384], P(None, 'narrow', 'wide')
- new_probe: float32 [4, 2, 256, 256], replicated
The draws below stay inside these ranges and needn't reach their ends.
Inputs may be any that keep to these rules, and one draw needn't show every extreme that they name: `offsets`: row 0: a window's top edge relative to the tile's margin-extended frame, at most 512; row 1: its left edge, at most 1024. Entries of slots that are not live carry no meaning. Live slots of a tile are its first counts slots; some tile holds 6 and some tile holds 1.
All inputs are finite; a program needn't handle non-finite values.
Results may differ from the reference program's by a relative error of at most 0.0001.
Values sent between devices are 32-bit elements; how exact they have to be, the bound alone decides.
No kernel may reach another device: no remote copies, remote signals or barrier semaphores. Data moves between devices by JAX's collectives and lax.ppermute only.
A program may use at most 128 MiB of HBM per device.

```python
import math
import jax
import jax.numpy as jnp
from jax import lax

PATCH = 256
MODES = 4
TILE_R = 512
TILE_C = 1024
CAP = 6
HALO = 128
NROWS = 4096
NCOLS = 16384
N_WIDE = 16
N_NARROW = 8


def draw_offsets(key, part):
    key = jax.random.fold_in(key, 11)
    key_rows, key_cols = jax.random.split(key, 2)
    row_most = TILE_R + 2 * HALO - PATCH
    col_most = TILE_C + 2 * HALO - PATCH
    rows_drawn = jax.random.randint(key_rows, (N_NARROW, N_WIDE, CAP), 0, row_most + 1)
    cols_drawn = jax.random.randint(key_cols, (N_NARROW, N_WIDE, CAP), 0, col_most + 1)
    rows_drawn = rows_drawn.at[0, 0, 0].set(row_most).at[N_NARROW - 1, N_WIDE - 1, 0].set(0)
    cols_drawn = cols_drawn.at[0, 0, 0].set(col_most).at[N_NARROW - 1, N_WIDE - 1, 0].set(0)
    return jnp.stack([rows_drawn, cols_drawn]).astype(jnp.int32)


def draw_counts(key, part):
    key = jax.random.fold_in(key, 23)
    key_base, key_dense, key_column = jax.random.split(key, 3)
    base_counts = jax.random.randint(key_base, (N_NARROW, N_WIDE), 1, CAP // 2 + 2)
    dense_tiles = jax.random.randint(key_dense, (N_NARROW, N_WIDE), 0, 4) == 0
    filled = jnp.where(dense_tiles, CAP, base_counts)
    column = jax.random.randint(key_column, (), 0, N_WIDE)
    filled = filled.at[0, column].set(CAP)
    filled = filled.at[N_NARROW - 1, column].set(1)
    return filled.astype(jnp.int32)


def block_scale(stream_key, shape, pieces, low, largest):
    factor_of = 1.0
    for axis_at, blocks in pieces:
        heights = jax.random.uniform(jax.random.fold_in(jax.random.fold_in(stream_key, 6), axis_at), (blocks,), jnp.float32, low / len(pieces), largest / len(pieces))
        factor_of = factor_of * jnp.repeat(jnp.exp(heights), shape[axis_at] // blocks).reshape((-1,) + (1,) * (len(shape) - 1 - axis_at))
    return factor_of


def noise(own_key, dims, spread, limit, cuts=(), held_as=jnp.bfloat16):
    gain = block_scale(own_key, dims, cuts, -0.22, 0.18) if cuts else 1.0
    entries = jax.random.normal(own_key, dims, jnp.float32) * spread * gain
    return jnp.minimum(jnp.maximum(entries, -limit), limit).astype(held_as)


def setup_inputs(seed: int = 0) -> dict:
    seeds = jax.random.split(jax.random.key(seed), 6)
    return {
        "object_field": noise(seeds[0], (2, NROWS, NCOLS), 1.0, 6.0, ((1, 8), (2, 16)), jnp.float32),
        "probe_modes": noise(seeds[1], (MODES, 2, PATCH, PATCH), 0.5, 4.0, (), jnp.float32),
        "amplitudes": jnp.clip(jnp.exp(math.log(4.0) - 2.0794415 * jax.random.uniform(seeds[2], (N_NARROW, N_WIDE, CAP, PATCH, PATCH), jnp.float32) ** block_scale(seeds[2], (N_NARROW, N_WIDE, CAP, PATCH, PATCH), ((0, 8), (1, 16)), -0.2, 0.2)), 0.5, 4.0),
        "offsets": draw_offsets(jax.random.fold_in(seeds[5], 71), 0),
        "counts": draw_counts(jax.random.fold_in(seeds[5], 71), 0),
    }


amp_floor = 0.25
step_floor = 1.0

def reference(object_field, probe_modes, amplitudes, offsets, counts):
    padded = jnp.pad(object_field, ((0, 0), (HALO, HALO), (HALO, HALO)))
    illum_one = lax.optimization_barrier(jnp.sum(probe_modes * probe_modes, axis=(0, 1)))
    probe_cplx = probe_modes[:, 0] + 1j * probe_modes[:, 1]
    totals = jnp.zeros((3, padded.shape[1], padded.shape[2]), jnp.float32)
    probe_sum = jnp.zeros(probe_modes.shape, jnp.float32)
    power_sum = jnp.zeros((PATCH, PATCH), jnp.float32)

    def visit_one(counter, carry):
        totals, probe_sum, power_sum = carry
        counter = jnp.asarray(counter).astype(jnp.int32)
        tile_row = counter // (N_WIDE * CAP)
        tile_col = counter // CAP % N_WIDE
        slot_index = counter % CAP
        is_live = (slot_index < counts[tile_row, tile_col]).astype(jnp.float32)
        top_row = (tile_row * TILE_R + offsets[0, tile_row, tile_col, slot_index]).astype(jnp.int32)
        left_col = (tile_col * TILE_C + offsets[1, tile_row, tile_col, slot_index]).astype(jnp.int32)
        zero_idx = jnp.zeros((), jnp.int32)
        window = lax.dynamic_slice(padded, (zero_idx, top_row, left_col), (2, PATCH, PATCH))
        measured = amplitudes[tile_row, tile_col, slot_index]
        cells = window[0] + 1j * window[1]
        wave = probe_cplx * cells[None]
        far_field = jnp.fft.fft2(wave, norm='ortho')
        intensity = lax.optimization_barrier(jnp.sum(jnp.real(far_field) ** 2 + jnp.imag(far_field) ** 2, axis=0))
        model_amp = jnp.sqrt(intensity + amp_floor)
        chi_field = far_field * (1.0 - measured / model_amp)[None]
        back_field = jnp.fft.ifft2(chi_field, norm='ortho')
        obj_grad = lax.optimization_barrier(jnp.sum(jnp.conj(probe_cplx) * back_field, axis=0))
        probe_grad = jnp.conj(cells)[None] * back_field
        patch_power = window[0] * window[0] + window[1] * window[1]
        stacked = jnp.stack([jnp.real(obj_grad), jnp.imag(obj_grad), illum_one]).astype(totals.dtype) * is_live
        current = lax.dynamic_slice(totals, (zero_idx, top_row, left_col), (3, PATCH, PATCH))
        totals = lax.dynamic_update_slice(totals, current + stacked, (zero_idx, top_row, left_col))
        grad_parts = jnp.stack([jnp.real(probe_grad), jnp.imag(probe_grad)], axis=1).astype(probe_sum.dtype)
        probe_sum = probe_sum + grad_parts * is_live
        power_sum = power_sum + patch_power * is_live
        return (totals, probe_sum, power_sum)
    totals, probe_sum, power_sum = lax.fori_loop(0, N_NARROW * N_WIDE * CAP, visit_one, (totals, probe_sum, power_sum))
    inner = totals[:, HALO:HALO + NROWS, HALO:HALO + NCOLS]
    new_object = object_field - inner[:2] / (inner[2] + step_floor)
    new_probe = probe_modes - probe_sum / (power_sum + step_floor)
    return (new_object, new_probe)
```

```python
import functools

import jax
import jax.numpy as jnp
import numpy as np
from jax import lax
from jax.experimental import pallas as pl
from jax.experimental.pallas import tpu as pltpu
from jax.sharding import PartitionSpec as P

amp_floor = 0.25
step_floor = 1.0
F32 = jnp.float32
BF16 = jnp.bfloat16
BOTH = ("wide", "narrow")
MIB = 1024 * 1024


def tables(length):
    half = length // 2
    row = np.arange(half)[:, None]
    col = np.arange(half)[None, :]
    pairs = []
    for odd in (0, 1):
        angle = -2.0 * np.pi * (row * (2 * col + odd) % length) / length
        re = np.cos(angle) / np.sqrt(length)
        im = np.sin(angle) / np.sqrt(length)
        matrix = np.block([[re, im], [-im, re]]).astype(np.float32)
        for table in (matrix, matrix.T):
            high = table.astype(jnp.bfloat16)
            low = (table - high.astype(np.float32)).astype(jnp.bfloat16)
            pairs.append((high, low))
    m0, m0t, m1, m1t = pairs
    after = np.stack([np.concatenate([h, h, l], 0) for h, l in (m0, m1, m0t, m1t)])
    before = np.stack([np.concatenate([h, h, l], 1) for h, l in (m0t, m1t, m0, m1)])
    order = np.zeros((length, length), np.float32)
    for k in range(half):
        order[2 * k, k] = 1
        order[2 * k + 1, half + k] = 1
    order = np.concatenate([order, order], 0).astype(jnp.bfloat16)
    return jnp.asarray(after), jnp.asarray(before), jnp.asarray(order)


def split(x):
    high = x.astype(BF16)
    return high, (x - high.astype(F32)).astype(BF16)


def dot(a, b):
    return jnp.dot(a, b, preferred_element_type=F32)


def grads_kernel(
    count, offs, obj, left, right, up, down, cup, cdown, probe, amps, after, before, order,
    core_o, left_o, right_o, up_o, down_o, cup_o, cdown_o, pg,
    ext, tot, win, zs, zd, p0, p1, u, ap, illum, sems, *, modes, n, tr, tc,
):
    h = n // 2
    ch = 64
    nb = ch // 8

    def places(big, core, left, right, up, down, cup, cdown):
        rows, cols = pl.ds(h, tr), pl.ds(h, tc)
        lo, hi = pl.ds(0, h), pl.ds(h + tc, h)
        top, bot = pl.ds(0, h), pl.ds(h + tr, h)
        return [
            (core, big.at[:, rows, cols]),
            (left, big.at[:, rows, lo]),
            (right, big.at[:, rows, hi]),
            (up, big.at[:, top, cols]),
            (down, big.at[:, bot, cols]),
            (cup.at[0], big.at[:, top, lo]),
            (cup.at[1], big.at[:, top, hi]),
            (cdown.at[0], big.at[:, bot, lo]),
            (cdown.at[1], big.at[:, bot, hi]),
        ]

    loads = [
        pltpu.make_async_copy(a, b, sems.at[i])
        for i, (a, b) in enumerate(places(ext, obj, left, right, up, down, cup, cdown))
    ]
    for copy in loads:
        copy.start()
    tot[...] = jnp.zeros_like(tot)
    pg[...] = jnp.zeros_like(pg)
    for r0 in range(0, n, ch):
        rs = pl.ds(r0, ch)
        acc = jnp.zeros((ch, n), F32)
        for k in range(modes):
            for c in range(2):
                v = probe[k, c, rs, :]
                acc = acc + v * v
        illum[rs, :] = acc
    for copy in loads:
        copy.wait()

    lane = lax.broadcasted_iota(jnp.int32, (ch + 8, h), 1)
    sub = lax.broadcasted_iota(jnp.int32, (nb, 8, h), 1)
    sub9 = lax.broadcasted_iota(jnp.int32, (nb + 1, 8, h), 1)

    def after_dot(z, i):
        return dot(jnp.concatenate([z[...], z[:, :n]], axis=1), after[i])

    def before_dot(i, y):
        high, low = split(y)
        return dot(before[i], jnp.concatenate([high, low, high], axis=0))

    def slot(s, carry):
        r = offs[0, s]
        c = offs[1, s]
        q = jnp.minimum(c // h, (ext.shape[2] - 3 * h) // h)
        rem = c - q * h
        q = pl.multiple_of(q * h, h)
        back_lanes = jnp.where((rem == 0) | (rem == h), 0, h - rem)
        fwd_lanes = jnp.where(rem == h, 0, rem)
        r8 = jnp.minimum(r // 8, (ext.shape[1] - n - 8) // 8)
        rr = r - r8 * 8
        r8 = pl.multiple_of(r8 * 8, 8)
        back_rows = jnp.where((rr == 0) | (rr == 8), 0, 8 - rr)
        fwd_rows = jnp.where(rr == 8, 0, rr)
        for r0 in range(0, n, ch):
            rs = pl.ds(r0, ch)
            w = []
            for comp in range(2):
                blk = ext[comp, pl.ds(r8 + r0, ch + 8), pl.ds(q, 3 * h)]
                t = [pltpu.roll(blk[:, j * h : (j + 1) * h], back_lanes, axis=1) for j in range(3)]
                keep = lane < h - rem
                sides = []
                for x, y in ((t[0], t[1]), (t[1], t[2])):
                    g = jnp.where(keep, x, y).reshape(nb + 1, 8, h)
                    g = pltpu.roll(g, back_rows, axis=1)
                    sides.append(jnp.where(sub < 8 - rr, g[:-1], g[1:]).reshape(ch, h))
                v = jnp.concatenate(sides, axis=1)
                win[comp, rs, :] = v
                w.append(v)
            pg[pl.ds(r0 // 8, nb), 2 * modes] += (w[0] * w[0] + w[1] * w[1]).reshape(nb, 8, n)
        for k in range(modes):
            for r0 in range(0, n, ch):
                rs = pl.ds(r0, ch)
                ks = pl.ds(k * n + r0, ch)
                ar, ai = win[0, rs, :], win[1, rs, :]
                pr, pi = probe[k, 0, rs, :], probe[k, 1, rs, :]
                wr = pr * ar - pi * ai
                wi = pr * ai + pi * ar
                z = jnp.concatenate([wr[:, :h] + wr[:, h:], wi[:, :h] + wi[:, h:]], axis=1)
                zs[ks, :n], zs[ks, n:] = split(z)
                z = jnp.concatenate([wr[:, :h] - wr[:, h:], wi[:, :h] - wi[:, h:]], axis=1)
                zd[ks, :n], zd[ks, n:] = split(z)
        p0[...] = after_dot(zs, 0)
        p1[...] = after_dot(zd, 1)
        for k in range(modes):
            top, bot = pl.ds(k * n, h), pl.ds(k * n + h, h)

            def folded(sign):
                parts = []
                for ls in (slice(0, h), slice(h, n)):
                    parts.append(
                        jnp.concatenate([p[top, ls] + sign * p[bot, ls] for p in (p0, p1)], axis=1)
                    )
                return jnp.concatenate(parts, axis=0)

            u[k, 0] = before_dot(0, folded(1.0))
            u[k, 1] = before_dot(1, folded(-1.0))
        am = dot(jnp.concatenate(split(amps[s]), axis=1), order[...])
        ap[0] = am[:, :h]
        ap[1] = am[:, h:]
        factor = []
        for e in range(2):
            power = jnp.zeros((h, n), F32)
            for k in range(modes):
                a, b = u[k, e, :h, :], u[k, e, h:, :]
                power = power + (a * a + b * b)
            am = jnp.concatenate([ap[j, pl.ds(e, h, stride=2), :] for j in range(2)], axis=1)
            factor.append(1.0 - am * lax.rsqrt(power + amp_floor))
        for k in range(modes):
            y = [
                jnp.concatenate([u[k, e, :h, :] * factor[e], u[k, e, h:, :] * factor[e]], axis=0)
                for e in range(2)
            ]
            even, odd = before_dot(2, y[0]), before_dot(3, y[1])
            for half, v in ((0, even + odd), (1, even - odd)):
                ks = pl.ds(k * n + half * h, h)
                for ref, ls in ((zs, slice(0, h)), (zd, slice(h, n))):
                    z = jnp.concatenate([v[:h, ls], v[h:, ls]], axis=1)
                    ref[ks, :n], ref[ks, n:] = split(z)
        p0[...] = after_dot(zs, 2)
        p1[...] = after_dot(zd, 3)
        for r0 in range(0, n, ch):
            rs = pl.ds(r0, ch)
            bs = pl.ds(r0 // 8, nb)
            ar, ai = win[0, rs, :], win[1, rs, :]
            o_re = jnp.zeros((ch, n), F32)
            o_im = jnp.zeros((ch, n), F32)
            for k in range(modes):
                ks = pl.ds(k * n + r0, ch)
                e, o = p0[ks, :], p1[ks, :]
                lhs, rhs = e + o, e - o
                br = jnp.concatenate([lhs[:, :h], rhs[:, :h]], axis=1)
                bi = jnp.concatenate([lhs[:, h:], rhs[:, h:]], axis=1)
                pr, pi = probe[k, 0, rs, :], probe[k, 1, rs, :]
                o_re = o_re + (pr * br + pi * bi)
                o_im = o_im + (pr * bi - pi * br)
                pg[bs, 2 * k] += (ar * br + ai * bi).reshape(nb, 8, n)
                pg[bs, 2 * k + 1] += (ar * bi - ai * br).reshape(nb, 8, n)

            def lowered(v):
                g = pltpu.roll(v.reshape(nb, 8, h), fwd_rows, axis=1)
                zero = jnp.zeros((1, 8, h), F32)
                here = jnp.concatenate([g, zero], axis=0)
                above = jnp.concatenate([zero, g], axis=0)
                return jnp.where(sub9 >= rr, here, above).reshape(ch + 8, h)

            past = lane >= rem
            for comp, v in ((0, o_re), (1, o_im), (2, illum[rs, :])):
                t0 = pltpu.roll(lowered(v[:, :h]), fwd_lanes, axis=1)
                t1 = pltpu.roll(lowered(v[:, h:]), fwd_lanes, axis=1)
                zero = jnp.zeros_like(t0)
                full = [
                    jnp.where(past, t0, zero),
                    jnp.where(past, t1, t0),
                    jnp.where(past, zero, t1),
                ]
                tot[comp, pl.ds(r8 + r0, ch + 8), pl.ds(q, 3 * h)] += jnp.concatenate(full, axis=1)
        return carry

    lax.fori_loop(0, count[0], slot, 0)
    stores = [
        pltpu.make_async_copy(b, a, sems.at[i])
        for i, (a, b) in enumerate(
            places(tot, core_o, left_o, right_o, up_o, down_o, cup_o, cdown_o)
        )
    ]
    for copy in stores:
        copy.start()
    for copy in stores:
        copy.wait()


def tile_grads(count, offs, obj, halos, probe, amps):
    modes, _, n, _ = probe.shape
    h = n // 2
    _, tr, tc = obj.shape
    vmem = pl.BlockSpec(memory_space=pltpu.VMEM)
    smem = pl.BlockSpec(memory_space=pltpu.SMEM)
    anyw = pl.BlockSpec(memory_space=pl.ANY)
    shape = lambda *dims: jax.ShapeDtypeStruct(dims, F32)
    rows, cols = tr + n, tc + n
    return pl.pallas_call(
        functools.partial(grads_kernel, modes=modes, n=n, tr=tr, tc=tc),
        out_shape=(
            shape(3, tr, tc), shape(3, tr, h), shape(3, tr, h), shape(3, h, tc), shape(3, h, tc),
            shape(2, 3, h, h), shape(2, 3, h, h), shape(n // 8, 2 * modes + 1, 8, n),
        ),
        in_specs=[smem, smem] + [anyw] * 7 + [vmem] * 5,
        out_specs=[anyw] * 7 + [vmem],
        scratch_shapes=[
            pltpu.VMEM((2, rows, cols), F32),
            pltpu.VMEM((3, rows, cols), F32),
            pltpu.VMEM((2, n, n), F32),
            pltpu.VMEM((modes * n, 2 * n), BF16),
            pltpu.VMEM((modes * n, 2 * n), BF16),
            pltpu.VMEM((modes * n, n), F32),
            pltpu.VMEM((modes * n, n), F32),
            pltpu.VMEM((modes, 2, n, n), F32),
            pltpu.VMEM((2, n, h), F32),
            pltpu.VMEM((n, n), F32),
            pltpu.SemaphoreType.DMA((9,)),
        ],
        compiler_params=pltpu.CompilerParams(vmem_limit_bytes=56 * MIB),
        cost_estimate=pl.CostEstimate(flops=40_000_000_000, bytes_accessed=30_000_000, transcendentals=0),
        name="tile_grads",
    )(count, offs, obj, *halos, probe, amps, *tables(n))


def object_update(obj, core, left, right, up, down):
    h = left.shape[-1]
    total = core + jnp.pad(left, ((0, 0), (0, 0), (0, core.shape[2] - h)))
    total = total + jnp.pad(right, ((0, 0), (0, 0), (core.shape[2] - h, 0)))
    total = total + jnp.pad(up, ((0, 0), (0, core.shape[1] - h), (0, 0)))
    total = total + jnp.pad(down, ((0, 0), (core.shape[1] - h, 0), (0, 0)))
    return obj - total[:2] / (total[2] + step_floor)


def moved(block, axis, distance):
    count = lax.axis_size(axis)
    route = [(i, i + distance) for i in range(count) if 0 <= i + distance < count]
    return lax.ppermute(block, axis, route)


def place(flat):
    w, n = flat // 8, flat % 8
    return {"core": w % 2, "x": w // 4, "y": (n // 4) * 2 + (w // 2) % 2, "z": n % 4}


def flat_of(at):
    w = at["x"] * 4 + (at["y"] % 2) * 2 + at["core"]
    n = (at["y"] // 2) * 4 + at["z"]
    return w * 8 + n


def route(step):
    pairs = []
    for i in range(128):
        at = place(i)
        if step == "core":
            at["core"] ^= 1
        else:
            axis = step[at["core"]]
            at[axis] = at[axis] ^ 1 if step[2] == 0 else 3 - at[axis]
        pairs.append((i, flat_of(at)))
    return pairs


def probe_update(pg, probe):
    w, n = lax.axis_index("wide"), lax.axis_index("narrow")
    core, x, y = w % 2, w // 4, (n // 4) * 2 + (w // 2) % 2

    def bit(step):
        if step == "core":
            return core
        t = jnp.where(core == 0, {"x": x, "y": y}[step[0]], {"x": x, "y": y}[step[1]])
        high = t // 2
        return high ^ (t % 2) if step[2] == 0 else high

    steps = ["core", ("x", "y", 0), ("x", "y", 1), ("y", "x", 0), ("y", "x", 1)]
    v = pg
    block = jnp.zeros((), jnp.int32)
    for step in steps:
        half = v.shape[0] // 2
        b = bit(step)
        block = block * 2 + b
        give = lax.dynamic_slice_in_dim(v, (1 - b) * half, half, 0)
        keep = lax.dynamic_slice_in_dim(v, b * half, half, 0)
        v = keep + lax.ppermute(give, BOTH, route(step))
    for which in (0, 1):
        v = v + lax.ppermute(v, BOTH, route(("z", "z", which)))
    v = v[0]
    modes, _, size, _ = probe.shape
    mine = lax.dynamic_slice_in_dim(probe.reshape(2 * modes, size, size), block * 8, 8, 1)
    mine = mine - v[: 2 * modes] / (v[2 * modes] + step_floor)
    for step in reversed(steps):
        got = lax.ppermute(mine, BOTH, route(step))
        b = bit(step)
        mine = jnp.where(
            b == 0, jnp.concatenate([mine, got], 1), jnp.concatenate([got, mine], 1)
        )
    return mine.reshape(probe.shape)


def on_device(object_field, probe_modes, amplitudes, offsets, counts):
    h = probe_modes.shape[-1] // 2
    _, tr, tc = object_field.shape
    up = moved(object_field[:, tr - h :], "narrow", 1)
    down = moved(object_field[:, :h], "narrow", -1)
    left = moved(object_field[:, :, tc - h :], "wide", 1)
    right = moved(object_field[:, :, :h], "wide", -1)
    cup = moved(jnp.stack([left[:, tr - h :], right[:, tr - h :]]), "narrow", 1)
    cdown = moved(jnp.stack([left[:, :h], right[:, :h]]), "narrow", -1)
    core, left_g, right_g, up_g, down_g, cup_g, cdown_g, pg = tile_grads(
        counts[0], offsets[:, 0, 0], object_field, (left, right, up, down, cup, cdown),
        probe_modes, amplitudes[0, 0],
    )
    from_below = moved(up_g, "narrow", -1)
    from_above = moved(down_g, "narrow", 1)
    corner_below = moved(cup_g, "narrow", -1)
    corner_above = moved(cdown_g, "narrow", 1)
    sides = []
    for i, strip in enumerate((left_g, right_g)):
        strip = strip + jnp.pad(corner_above[i], ((0, 0), (0, tr - h), (0, 0)))
        strip = strip + jnp.pad(corner_below[i], ((0, 0), (tr - h, 0), (0, 0)))
        sides.append(strip)
    from_right = moved(sides[0], "wide", -1)
    from_left = moved(sides[1], "wide", 1)
    new_probe = probe_update(pg, probe_modes)
    new_object = object_update(object_field, core, from_left, from_right, from_above, from_below)
    return (new_object, new_probe)


def solution(mesh):
    return jax.shard_map(
        on_device,
        mesh=mesh,
        in_specs=(
            P(None, "narrow", "wide"),
            P(),
            P("narrow", "wide", None, None, None),
            P(None, "narrow", "wide", None),
            P("narrow", "wide"),
        ),
        out_specs=(P(None, "narrow", "wide"), P()),
        check_vma=False,
    )
```

```python
import functools

import jax
import jax.numpy as jnp
import numpy as np
from jax import lax
from jax.experimental import pallas as pl
from jax.experimental.pallas import tpu as pltpu
from jax.sharding import PartitionSpec as P

amp_floor = 0.25
step_floor = 1.0
F32 = jnp.float32
BF16 = jnp.bfloat16
BOTH = ("wide", "narrow")
MIB = 1024 * 1024


def tables(length):
    half = length // 2
    row = np.arange(half)[:, None]
    col = np.arange(half)[None, :]
    pairs = []
    for odd in (0, 1):
        angle = -2.0 * np.pi * (row * (2 * col + odd) % length) / length
        re = np.cos(angle) / np.sqrt(length)
        im = np.sin(angle) / np.sqrt(length)
        matrix = np.block([[re, im], [-im, re]]).astype(np.float32)
        for table in (matrix, matrix.T):
            high = table.astype(jnp.bfloat16)
            low = (table - high.astype(np.float32)).astype(jnp.bfloat16)
            pairs.append((high, low))
    m0, m0t, m1, m1t = pairs
    after = np.stack([np.concatenate([h, h, l], 0) for h, l in (m0, m1, m0t, m1t)])
    before = np.stack([np.concatenate([h, h, l], 1) for h, l in (m0t, m1t, m0, m1)])
    order = np.zeros((length, length), np.float32)
    for k in range(half):
        order[2 * k, k] = 1
        order[2 * k + 1, half + k] = 1
    order = np.concatenate([order, order], 0).astype(jnp.bfloat16)
    return jnp.asarray(after), jnp.asarray(before), jnp.asarray(order)


def split(x):
    high = x.astype(BF16)
    return high, (x - high.astype(F32)).astype(BF16)


def dot(a, b):
    return jnp.dot(a, b, preferred_element_type=F32)


def add_shifted(tot, comp, v, r0, r8, rr, q, rem):
    ch, n = v.shape
    h, nb = n // 2, ch // 8
    fwd_lanes = jnp.where(rem == h, 0, rem)
    fwd_rows = jnp.where(rr == 8, 0, rr)
    past = lax.broadcasted_iota(jnp.int32, (ch + 8, h), 1) >= rem
    below = lax.broadcasted_iota(jnp.int32, (nb + 1, 8, h), 1) >= rr

    def lowered(v):
        g = pltpu.roll(v.reshape(nb, 8, h), fwd_rows, axis=1)
        zero = jnp.zeros((1, 8, h), F32)
        here = jnp.concatenate([g, zero], axis=0)
        above = jnp.concatenate([zero, g], axis=0)
        return pltpu.roll(jnp.where(below, here, above).reshape(ch + 8, h), fwd_lanes, axis=1)

    t0, t1 = lowered(v[:, :h]), lowered(v[:, h:])
    zero = jnp.zeros_like(t0)
    full = [jnp.where(past, t0, zero), jnp.where(past, t1, t0), jnp.where(past, zero, t1)]
    tot[comp, pl.ds(r8 + r0, ch + 8), pl.ds(q, 3 * h)] += jnp.concatenate(full, axis=1)


def window_place(offs, s, rows, cols, n):
    h = n // 2
    r, c = offs[0, s], offs[1, s]
    q = jnp.minimum(c // h, (cols - 3 * h) // h)
    rem = c - q * h
    r8 = jnp.minimum(r // 8, (rows - n - 8) // 8)
    rr = r - r8 * 8
    return pl.multiple_of(r8 * 8, 8), rr, pl.multiple_of(q * h, h), rem


def copies(pairs, sems):
    return [pltpu.make_async_copy(a, b, sems.at[i]) for i, (a, b) in enumerate(pairs)]


def illum_kernel(info, probe, out, tot, one, *, modes, n, tr, tc, slots):
    h, ch = n // 2, 64
    tot[...] = jnp.zeros_like(tot)
    for r0 in range(0, n, ch):
        rs = pl.ds(r0, ch)
        acc = jnp.zeros((ch, n), F32)
        for k in range(modes):
            for c in range(2):
                v = probe[k, c, rs, :]
                acc = acc + v * v
        one[rs, :] = acc

    def visit(i, carry):
        t, s = i // slots, i % slots
        live = s < info[t, 0]
        r = jnp.where(live, info[t, 1 + s], 0) + (t // 3 - 1) * tr + h
        c = jnp.where(live, info[t, 1 + slots + s], 0) + (t % 3 - 1) * tc + h

        @pl.when(live & (r > 0) & (r < tr + n) & (c > 0) & (c < tc + n))
        def _():
            r8 = pl.multiple_of(r // 8 * 8, 8)
            q = pl.multiple_of(c // h * h, h)
            for r0 in range(0, n, ch):
                add_shifted(tot, 0, one[pl.ds(r0, ch), :], r0, r8, r - r8, q, c - q)

        return carry

    lax.fori_loop(0, 9 * slots, visit, 0)
    out[...] = tot[0, n : n + tr, n : n + tc] + step_floor


def tile_illum(info, probe, tr, tc, slots):
    modes, _, n, _ = probe.shape
    vmem = pl.BlockSpec(memory_space=pltpu.VMEM)
    smem = pl.BlockSpec(memory_space=pltpu.SMEM)
    return pl.pallas_call(
        functools.partial(illum_kernel, modes=modes, n=n, tr=tr, tc=tc, slots=slots),
        out_shape=jax.ShapeDtypeStruct((tr, tc), F32),
        in_specs=[smem, vmem],
        out_specs=vmem,
        scratch_shapes=[pltpu.VMEM((1, tr + 2 * n, tc + 2 * n), F32), pltpu.VMEM((n, n), F32)],
        compiler_params=pltpu.CompilerParams(vmem_limit_bytes=16 * MIB),
        cost_estimate=pl.CostEstimate(flops=20_000_000, bytes_accessed=8_000_000, transcendentals=0),
        name="tile_illum",
    )(info, probe)


def grads_kernel(
    count, offs, bit, obj, left, right, up, down, probe, amps, after, before, order,
    core_o, left_o, right_o, up_o, down_o, give_o, keep_o,
    ext, tot, pg, win, zs, zd, p0, p1, u, ap, sems, *, modes, n, tr, tc,
):
    h = n // 2
    ch = 64
    nb = ch // 8

    def places(big, core, left, right, up, down):
        rows = pl.ds(h, tr)
        return [
            (core, big.at[:, rows, pl.ds(h, tc)]),
            (left.at[:, pl.ds(0, tr), :], big.at[:, rows, pl.ds(0, h)]),
            (right.at[:, pl.ds(0, tr), :], big.at[:, rows, pl.ds(h + tc, h)]),
            (up.at[:, pl.ds(0, h), :], big.at[:, pl.ds(0, h), :]),
            (down.at[:, pl.ds(0, h), :], big.at[:, pl.ds(h + tr, h), :]),
        ]

    loads = copies(places(ext, obj, left, right, up, down), sems)
    for copy in loads:
        copy.start()
    tot[...] = jnp.zeros_like(tot)
    pg[...] = jnp.zeros_like(pg)
    for copy in loads:
        copy.wait()

    lane = lax.broadcasted_iota(jnp.int32, (ch + 8, h), 1)
    sub = lax.broadcasted_iota(jnp.int32, (nb, 8, h), 1)

    def after_dot(z, i):
        return dot(jnp.concatenate([z[...], z[:, :n]], axis=1), after[i])

    def before_dot(i, y):
        high, low = split(y)
        return dot(before[i], jnp.concatenate([high, low, high], axis=0))

    def slot(s, carry):
        r8, rr, q, rem = window_place(offs, s, tr + n, tc + n, n)
        back_lanes = jnp.where((rem == 0) | (rem == h), 0, h - rem)
        back_rows = jnp.where((rr == 0) | (rr == 8), 0, 8 - rr)
        for r0 in range(0, n, ch):
            rs = pl.ds(r0, ch)
            w = []
            for comp in range(2):
                blk = ext[comp, pl.ds(r8 + r0, ch + 8), pl.ds(q, 3 * h)]
                t = [pltpu.roll(blk[:, j * h : (j + 1) * h], back_lanes, axis=1) for j in range(3)]
                keep = lane < h - rem
                sides = []
                for x, y in ((t[0], t[1]), (t[1], t[2])):
                    g = jnp.where(keep, x, y).reshape(nb + 1, 8, h)
                    g = pltpu.roll(g, back_rows, axis=1)
                    sides.append(jnp.where(sub < 8 - rr, g[:-1], g[1:]).reshape(ch, h))
                v = jnp.concatenate(sides, axis=1)
                win[comp, rs, :] = v
                w.append(v)
            pg[pl.ds(r0 // 8, nb), 2 * modes] += (w[0] * w[0] + w[1] * w[1]).reshape(nb, 8, n)
        for k in range(modes):
            for r0 in range(0, n, ch):
                rs = pl.ds(r0, ch)
                ks = pl.ds(k * n + r0, ch)
                ar, ai = win[0, rs, :], win[1, rs, :]
                pr, pi = probe[k, 0, rs, :], probe[k, 1, rs, :]
                wr = pr * ar - pi * ai
                wi = pr * ai + pi * ar
                z = jnp.concatenate([wr[:, :h] + wr[:, h:], wi[:, :h] + wi[:, h:]], axis=1)
                zs[ks, :n], zs[ks, n:] = split(z)
                z = jnp.concatenate([wr[:, :h] - wr[:, h:], wi[:, :h] - wi[:, h:]], axis=1)
                zd[ks, :n], zd[ks, n:] = split(z)
        p0[...] = after_dot(zs, 0)
        p1[...] = after_dot(zd, 1)
        for k in range(modes):
            top, bot = pl.ds(k * n, h), pl.ds(k * n + h, h)

            def folded(sign):
                parts = []
                for ls in (slice(0, h), slice(h, n)):
                    parts.append(
                        jnp.concatenate([p[top, ls] + sign * p[bot, ls] for p in (p0, p1)], axis=1)
                    )
                return jnp.concatenate(parts, axis=0)

            u[k, 0] = before_dot(0, folded(1.0))
            u[k, 1] = before_dot(1, folded(-1.0))
        am = dot(jnp.concatenate(split(amps[s]), axis=1), order[...])
        ap[0] = am[:, :h]
        ap[1] = am[:, h:]
        factor = []
        for e in range(2):
            power = jnp.zeros((h, n), F32)
            for k in range(modes):
                a, b = u[k, e, :h, :], u[k, e, h:, :]
                power = power + (a * a + b * b)
            am = jnp.concatenate([ap[j, pl.ds(e, h, stride=2), :] for j in range(2)], axis=1)
            factor.append(1.0 - am * lax.rsqrt(power + amp_floor))
        for k in range(modes):
            y = [
                jnp.concatenate([u[k, e, :h, :] * factor[e], u[k, e, h:, :] * factor[e]], axis=0)
                for e in range(2)
            ]
            even, odd = before_dot(2, y[0]), before_dot(3, y[1])
            for half, v in ((0, even + odd), (1, even - odd)):
                ks = pl.ds(k * n + half * h, h)
                for ref, ls in ((zs, slice(0, h)), (zd, slice(h, n))):
                    z = jnp.concatenate([v[:h, ls], v[h:, ls]], axis=1)
                    ref[ks, :n], ref[ks, n:] = split(z)
        p0[...] = after_dot(zs, 2)
        p1[...] = after_dot(zd, 3)
        for r0 in range(0, n, ch):
            rs = pl.ds(r0, ch)
            bs = pl.ds(r0 // 8, nb)
            ar, ai = win[0, rs, :], win[1, rs, :]
            o_re = jnp.zeros((ch, n), F32)
            o_im = jnp.zeros((ch, n), F32)
            for k in range(modes):
                ks = pl.ds(k * n + r0, ch)
                e, o = p0[ks, :], p1[ks, :]
                lhs, rhs = e + o, e - o
                br = jnp.concatenate([lhs[:, :h], rhs[:, :h]], axis=1)
                bi = jnp.concatenate([lhs[:, h:], rhs[:, h:]], axis=1)
                pr, pi = probe[k, 0, rs, :], probe[k, 1, rs, :]
                o_re = o_re + (pr * br + pi * bi)
                o_im = o_im + (pr * bi - pi * br)
                pg[bs, 2 * k] += (ar * br + ai * bi).reshape(nb, 8, n)
                pg[bs, 2 * k + 1] += (ar * bi - ai * br).reshape(nb, 8, n)

            for comp, v in ((0, o_re), (1, o_im)):
                add_shifted(tot, comp, v, r0, r8, rr, q, rem)
        return carry

    lax.fori_loop(0, count[0], slot, 0)
    half = n // 16
    give, keep = pl.ds((1 - bit[0]) * half, half), pl.ds(bit[0] * half, half)
    outs = [(pg.at[give], give_o), (pg.at[keep], keep_o)]
    outs += [(b, a) for a, b in places(tot, core_o, left_o, right_o, up_o, down_o)]
    stores = copies(outs, sems)
    for copy in stores:
        copy.start()
    for copy in stores:
        copy.wait()


def tile_grads(count, offs, bit, obj, halos, probe, amps):
    modes, _, n, _ = probe.shape
    h = n // 2
    _, tr, tc = obj.shape
    vmem = pl.BlockSpec(memory_space=pltpu.VMEM)
    smem = pl.BlockSpec(memory_space=pltpu.SMEM)
    anyw = pl.BlockSpec(memory_space=pl.ANY)
    shape = lambda *dims: jax.ShapeDtypeStruct(dims, F32)
    rows, cols = tr + n, tc + n
    return pl.pallas_call(
        functools.partial(grads_kernel, modes=modes, n=n, tr=tr, tc=tc),
        out_shape=(
            shape(2, tr, tc), shape(2, tr, h), shape(2, tr, h), shape(2, h, cols), shape(2, h, cols),
            shape(n // 16, 2 * modes + 1, 8, n), shape(n // 16, 2 * modes + 1, 8, n),
        ),
        in_specs=[smem, smem, smem] + [anyw] * 5 + [vmem] * 5,
        out_specs=[anyw] * 7,
        scratch_shapes=[
            pltpu.VMEM((2, rows, cols), F32),
            pltpu.VMEM((2, rows, cols), F32),
            pltpu.VMEM((n // 8, 2 * modes + 1, 8, n), F32),
            pltpu.VMEM((2, n, n), F32),
            pltpu.VMEM((modes * n, 2 * n), BF16),
            pltpu.VMEM((modes * n, 2 * n), BF16),
            pltpu.VMEM((modes * n, n), F32),
            pltpu.VMEM((modes * n, n), F32),
            pltpu.VMEM((modes, 2, n, n), F32),
            pltpu.VMEM((2, n, h), F32),
            pltpu.SemaphoreType.DMA((7,)),
        ],
        compiler_params=pltpu.CompilerParams(vmem_limit_bytes=56 * MIB),
        cost_estimate=pl.CostEstimate(flops=40_000_000_000, bytes_accessed=30_000_000, transcendentals=0),
        name="tile_grads",
    )(count, offs, bit, obj, *halos, probe, amps, *tables(n))


def object_update(obj, core, illum, left, right, above, below):
    _, tr, tc = obj.shape
    h = left.shape[-1]
    total = core + jnp.pad(left, ((0, 0), (0, 0), (0, tc - h)))
    total = total + jnp.pad(right, ((0, 0), (0, 0), (tc - h, 0)))
    total = total + jnp.pad(above[:, :, h : h + tc], ((0, 0), (0, tr - h), (0, 0)))
    total = total + jnp.pad(below[:, :, h : h + tc], ((0, 0), (tr - h, 0), (0, 0)))
    return obj - total / illum


def moved(block, axis, distance):
    count = lax.axis_size(axis)
    route = [(i, i + distance) for i in range(count) if 0 <= i + distance < count]
    return lax.ppermute(block, axis, route)


def place(flat):
    w, n = flat // 8, flat % 8
    return {"core": w % 2, "x": w // 4, "y": (n // 4) * 2 + (w // 2) % 2, "z": n % 4}


def flat_of(at):
    w = at["x"] * 4 + (at["y"] % 2) * 2 + at["core"]
    n = (at["y"] // 2) * 4 + at["z"]
    return w * 8 + n


def route(axes, hop):
    pairs = []
    for i in range(128):
        at = place(i)
        axis = axes[at["core"]]
        at[axis] = (at[axis] + hop) % (2 if axis == "core" else 4)
        pairs.append((i, flat_of(at)))
    return pairs


def around(piece, axes):
    return [lax.ppermute(piece, BOTH, route(axes, hop)) for hop in (1, 2, 3)]


def own_core():
    return lax.axis_index("wide") & 1


def probe_update(give, keep, probe, arrived, ready):
    w, n = lax.axis_index("wide"), lax.axis_index("narrow")
    core, x, y = w & 1, w >> 2, ((n >> 2) << 1) | ((w >> 1) & 1)
    v = keep + lax.ppermute(give, BOTH, route(("core", "core"), 1))

    def scattered(v, t, axis):
        size = v.shape[0] // 4
        part = lambda d: lax.dynamic_slice_in_dim(v, (d & 3) * size, size, 0)
        got = [
            lax.ppermute(part(t + hop), BOTH, route((axis, axis), hop)) for hop in (1, 2, 3)
        ]
        return part(t) + got[0] + got[1] + got[2]

    v = scattered(v, x, "x")
    v, arrived = lax.optimization_barrier((v, arrived))
    v = scattered(v, y, "y")
    a, b, c = around(v, ("z", "z"))
    v = (v + a + b + c)[0]
    modes, _, size, _ = probe.shape
    block = core * 16 + x * 4 + y
    mine = lax.dynamic_slice_in_dim(probe.reshape(2 * modes, size, size), block * 8, 8, 1)
    mine = mine - v[: 2 * modes] / (v[2 * modes] + step_floor)

    def gathered(piece, t, axes):
        pieces = [piece, *around(piece, axes)]
        rows = []
        for d in range(4):
            j = (t - d) & 3
            one = jnp.where(j < 2, jnp.where(j == 0, *pieces[:2]), jnp.where(j == 2, *pieces[2:]))
            rows.append(one)
        return jnp.concatenate(rows, axis=1)

    mine, ready = lax.optimization_barrier((mine, ready))
    mine = gathered(mine, jnp.where(core == 0, y, x), ("y", "x"))
    mine = gathered(mine, jnp.where(core == 0, x, y), ("x", "y"))
    got = lax.ppermute(mine, BOTH, route(("core", "core"), 1))
    first = jnp.where(core == 0, mine, got)
    second = jnp.where(core == 0, got, mine)
    second = second.reshape(2 * modes, 4, 4, 8, size).swapaxes(1, 2).reshape(first.shape)
    return jnp.concatenate([first, second], axis=1).reshape(probe.shape), arrived, ready


def label(count, offs, width):
    info = jnp.concatenate([count, offs[0], offs[1]]).astype(F32)
    info = jnp.pad(info, (0, width - info.shape[0]))
    return jnp.broadcast_to(info, (2, 8, width))


def on_device(object_field, probe_modes, amplitudes, offsets, counts):
    h = probe_modes.shape[-1] // 2
    _, tr, tc = object_field.shape
    count, offs = counts[0], offsets[:, 0, 0]
    mine = label(count, offs, h)
    tagged = lambda cols: jnp.concatenate([object_field[:, :, cols], mine], axis=1)
    left = moved(tagged(slice(tc - h, tc)), "wide", 1)
    right = moved(tagged(slice(0, h)), "wide", -1)
    own = jnp.concatenate([object_field, label(count, offs, tc)], axis=1)

    def wider(rows):
        parts = [left, own, right]
        return jnp.concatenate(
            [jnp.concatenate([p[:, rows], p[:, tr:]], axis=1) for p in parts], axis=2
        )

    up = moved(wider(slice(tr - h, tr)), "narrow", 1)
    down = moved(wider(slice(0, h)), "narrow", -1)
    pick = lambda a, row, col: a[0, row, col : col + 16]
    info = [pick(up, h, c) for c in (0, h, h + tc)]
    info += [pick(left, tr, 0), pick(own, tr, 0), pick(right, tr, 0)]
    info += [pick(down, h, c) for c in (0, h, h + tc)]
    info = jnp.stack(info).astype(jnp.int32)
    illum = tile_illum(info, probe_modes, tr, tc, offs.shape[-1])
    core, left_g, right_g, up_g, down_g, give, keep = tile_grads(
        count, offs, own_core()[None], object_field, (left, right, up, down),
        probe_modes, amplitudes[0, 0],
    )
    below = moved(up_g, "narrow", -1)
    above = moved(down_g, "narrow", 1)
    new_probe, (above, below), illum = probe_update(give, keep, probe_modes, (above, below), illum)
    side = lambda strip, cols: (
        strip
        + jnp.pad(above[:, :, cols], ((0, 0), (0, tr - h), (0, 0)))
        + jnp.pad(below[:, :, cols], ((0, 0), (tr - h, 0), (0, 0)))
    )
    from_right = moved(side(left_g, slice(0, h)), "wide", -1)
    from_left = moved(side(right_g, slice(h + tc, 2 * h + tc)), "wide", 1)
    new_object = object_update(object_field, core, illum, from_left, from_right, above, below)
    return (new_object, new_probe)


def solution(mesh):
    return jax.shard_map(
        on_device,
        mesh=mesh,
        in_specs=(
            P(None, "narrow", "wide"),
            P(),
            P("narrow", "wide", None, None, None),
            P(None, "narrow", "wide", None),
            P("narrow", "wide"),
        ),
        out_specs=(P(None, "narrow", "wide"), P()),
        check_vma=False,
    )
```

```python
import functools

import jax
import jax.numpy as jnp
import numpy as np
from jax import lax
from jax.experimental import pallas as pl
from jax.experimental.pallas import tpu as pltpu
from jax.sharding import PartitionSpec as P

amp_floor = 0.25
step_floor = 1.0
F32 = jnp.float32
BF16 = jnp.bfloat16
BOTH = ("wide", "narrow")
MIB = 1024 * 1024


def tables(length):
    half = length // 2
    row = np.arange(half)[:, None]
    col = np.arange(half)[None, :]
    pairs = []
    for odd in (0, 1):
        angle = -2.0 * np.pi * (row * (2 * col + odd) % length) / length
        re = np.cos(angle) / np.sqrt(length)
        im = np.sin(angle) / np.sqrt(length)
        matrix = np.block([[re, im], [-im, re]]).astype(np.float32)
        for table in (matrix, matrix.T):
            high = table.astype(jnp.bfloat16)
            low = (table - high.astype(np.float32)).astype(jnp.bfloat16)
            pairs.append((high, low))
    both = np.stack([np.stack(pair) for pair in pairs])
    order = np.zeros((length, length), np.float32)
    for k in range(half):
        order[2 * k, k] = 1
        order[2 * k + 1, half + k] = 1
    order = np.concatenate([order, order], 0).astype(jnp.bfloat16)
    return jnp.asarray(both), jnp.asarray(order)


def split(x):
    high = x.astype(BF16)
    return high, (x - high.astype(F32)).astype(BF16)


def dot(a, b):
    return jnp.dot(a, b, preferred_element_type=F32)


def add_shifted(tot, comp, v, r0, r8, rr, q, rem):
    ch, n = v.shape
    h, nb = n // 2, ch // 8
    fwd_lanes = jnp.where(rem == h, 0, rem)
    fwd_rows = jnp.where(rr == 8, 0, rr)
    past = lax.broadcasted_iota(jnp.int32, (ch + 8, h), 1) >= rem
    below = lax.broadcasted_iota(jnp.int32, (nb + 1, 8, h), 1) >= rr

    def lowered(v):
        g = pltpu.roll(v.reshape(nb, 8, h), fwd_rows, axis=1)
        zero = jnp.zeros((1, 8, h), F32)
        here = jnp.concatenate([g, zero], axis=0)
        above = jnp.concatenate([zero, g], axis=0)
        return pltpu.roll(jnp.where(below, here, above).reshape(ch + 8, h), fwd_lanes, axis=1)

    t0, t1 = lowered(v[:, :h]), lowered(v[:, h:])
    zero = jnp.zeros_like(t0)
    full = [jnp.where(past, t0, zero), jnp.where(past, t1, t0), jnp.where(past, zero, t1)]
    tot[comp, pl.ds(r8 + r0, ch + 8), pl.ds(q, 3 * h)] += jnp.concatenate(full, axis=1)


def window_place(offs, s, rows, cols, n):
    h = n // 2
    r, c = offs[0, s], offs[1, s]
    q = jnp.minimum(c // h, (cols - 3 * h) // h)
    rem = c - q * h
    r8 = jnp.minimum(r // 8, (rows - n - 8) // 8)
    rr = r - r8 * 8
    return pl.multiple_of(r8 * 8, 8), rr, pl.multiple_of(q * h, h), rem


def copies(pairs, sems):
    return [pltpu.make_async_copy(a, b, sems.at[i]) for i, (a, b) in enumerate(pairs)]


def illum_kernel(info, probe, out, tot, one, *, modes, n, tr, tc, slots):
    h, ch = n // 2, 64
    tot[...] = jnp.zeros_like(tot)
    for r0 in range(0, n, ch):
        rs = pl.ds(r0, ch)
        acc = jnp.zeros((ch, n), F32)
        for k in range(modes):
            for c in range(2):
                v = probe[k, c, rs, :]
                acc = acc + v * v
        one[rs, :] = acc

    def visit(i, carry):
        t, s = i // slots, i % slots
        live = s < info[t, 0]
        r = jnp.where(live, info[t, 1 + s], 0) + (t // 3 - 1) * tr + h
        c = jnp.where(live, info[t, 1 + slots + s], 0) + (t % 3 - 1) * tc + h

        @pl.when(live & (r > 0) & (r < tr + n) & (c > 0) & (c < tc + n))
        def _():
            r8 = pl.multiple_of(r // 8 * 8, 8)
            q = pl.multiple_of(c // h * h, h)
            for r0 in range(0, n, ch):
                add_shifted(tot, 0, one[pl.ds(r0, ch), :], r0, r8, r - r8, q, c - q)

        return carry

    lax.fori_loop(0, 9 * slots, visit, 0)
    out[...] = tot[0, n : n + tr, n : n + tc] + step_floor


def tile_illum(info, probe, tr, tc, slots):
    modes, _, n, _ = probe.shape
    vmem = pl.BlockSpec(memory_space=pltpu.VMEM)
    smem = pl.BlockSpec(memory_space=pltpu.SMEM)
    return pl.pallas_call(
        functools.partial(illum_kernel, modes=modes, n=n, tr=tr, tc=tc, slots=slots),
        out_shape=jax.ShapeDtypeStruct((tr, tc), F32),
        in_specs=[smem, vmem],
        out_specs=vmem,
        scratch_shapes=[pltpu.VMEM((1, tr + 2 * n, tc + 2 * n), F32), pltpu.VMEM((n, n), F32)],
        compiler_params=pltpu.CompilerParams(vmem_limit_bytes=16 * MIB),
        cost_estimate=pl.CostEstimate(flops=20_000_000, bytes_accessed=8_000_000, transcendentals=0),
        name="tile_illum",
    )(info, probe)


def grads_kernel(*refs, modes, n, tr, tc, early):
    count, offs, bit, obj, left, right, *refs = refs
    if early:
        probe, amps, table, order, core_o, left_o, right_o, pg_o, *refs = refs
    else:
        up, down, eup, edown, pg_e, probe, amps, table, order, *refs = refs
        core_o, left_o, right_o, up_o, down_o, give_o, keep_o, *refs = refs
    ext, tot, pg, win, zs, zd, p0, p1, u, ap, sems = refs
    h = n // 2
    ch = 64
    nb = ch // 8
    rows, cols = pl.ds(h, tr), pl.ds(h, tc)
    lo, hi = pl.ds(0, h), pl.ds(h + tc, h)
    top, bot = pl.ds(0, h), pl.ds(h + tr, h)
    places_in = [
        (obj, ext.at[:, rows, cols]),
        (left.at[:, pl.ds(0, tr), :], ext.at[:, rows, lo]),
        (right.at[:, pl.ds(0, tr), :], ext.at[:, rows, hi]),
    ]
    if not early:
        places_in += [
            (up, ext.at[:, top, cols]),
            (down, ext.at[:, bot, cols]),
            (eup.at[0, :, lo, :], ext.at[:, top, lo]),
            (eup.at[1, :, lo, :], ext.at[:, top, hi]),
            (edown.at[0, :, lo, :], ext.at[:, bot, lo]),
            (edown.at[1, :, lo, :], ext.at[:, bot, hi]),
            (pg_e, pg),
        ]
    loads = copies(places_in, sems)
    for copy in loads:
        copy.start()
    tot[...] = jnp.zeros_like(tot)
    if early:
        pg[...] = jnp.zeros_like(pg)
    for copy in loads:
        copy.wait()

    lane = lax.broadcasted_iota(jnp.int32, (ch + 8, h), 1)
    sub = lax.broadcasted_iota(jnp.int32, (nb, 8, h), 1)

    def after_dot(z, i):
        high, low = table[i, 0], table[i, 1]
        return dot(z[:, :n], high) + (dot(z[:, n:], high) + dot(z[:, :n], low))

    def before_dot(i, y):
        high, low = split(y)
        return dot(table[i, 0], high) + (dot(table[i, 0], low) + dot(table[i, 1], high))

    def visit(s, carry):
        inside = (offs[0, s] >= h) & (offs[0, s] <= tr + h - n)
        pl.when(inside if early else ~inside)(lambda: slot(s))
        return carry

    def slot(s):
        r8, rr, q, rem = window_place(offs, s, tr + n, tc + n, n)
        back_lanes = jnp.where((rem == 0) | (rem == h), 0, h - rem)
        back_rows = jnp.where((rr == 0) | (rr == 8), 0, 8 - rr)
        for r0 in range(0, n, ch):
            rs = pl.ds(r0, ch)
            w = []
            for comp in range(2):
                blk = ext[comp, pl.ds(r8 + r0, ch + 8), pl.ds(q, 3 * h)]
                t = [pltpu.roll(blk[:, j * h : (j + 1) * h], back_lanes, axis=1) for j in range(3)]
                keep = lane < h - rem
                sides = []
                for x, y in ((t[0], t[1]), (t[1], t[2])):
                    g = jnp.where(keep, x, y).reshape(nb + 1, 8, h)
                    g = pltpu.roll(g, back_rows, axis=1)
                    sides.append(jnp.where(sub < 8 - rr, g[:-1], g[1:]).reshape(ch, h))
                v = jnp.concatenate(sides, axis=1)
                win[comp, rs, :] = v
                w.append(v)
            pg[pl.ds(r0 // 8, nb), 2 * modes] += (w[0] * w[0] + w[1] * w[1]).reshape(nb, 8, n)
        for k in range(modes):
            for r0 in range(0, n, ch):
                rs = pl.ds(r0, ch)
                ks = pl.ds(k * n + r0, ch)
                ar, ai = win[0, rs, :], win[1, rs, :]
                pr, pi = probe[k, 0, rs, :], probe[k, 1, rs, :]
                wr = pr * ar - pi * ai
                wi = pr * ai + pi * ar
                z = jnp.concatenate([wr[:, :h] + wr[:, h:], wi[:, :h] + wi[:, h:]], axis=1)
                zs[ks, :n], zs[ks, n:] = split(z)
                z = jnp.concatenate([wr[:, :h] - wr[:, h:], wi[:, :h] - wi[:, h:]], axis=1)
                zd[ks, :n], zd[ks, n:] = split(z)
        p0[...] = after_dot(zs, 0)
        p1[...] = after_dot(zd, 2)
        for k in range(modes):
            top, bot = pl.ds(k * n, h), pl.ds(k * n + h, h)

            def folded(sign):
                parts = []
                for ls in (slice(0, h), slice(h, n)):
                    parts.append(
                        jnp.concatenate([p[top, ls] + sign * p[bot, ls] for p in (p0, p1)], axis=1)
                    )
                return jnp.concatenate(parts, axis=0)

            u[k, 0] = before_dot(1, folded(1.0))
            u[k, 1] = before_dot(3, folded(-1.0))
        am = dot(jnp.concatenate(split(amps[s]), axis=1), order[...])
        ap[0] = am[:, :h]
        ap[1] = am[:, h:]
        factor = []
        for e in range(2):
            power = jnp.zeros((h, n), F32)
            for k in range(modes):
                a, b = u[k, e, :h, :], u[k, e, h:, :]
                power = power + (a * a + b * b)
            am = jnp.concatenate([ap[j, pl.ds(e, h, stride=2), :] for j in range(2)], axis=1)
            factor.append(1.0 - am * lax.rsqrt(power + amp_floor))
        for k in range(modes):
            y = [
                jnp.concatenate([u[k, e, :h, :] * factor[e], u[k, e, h:, :] * factor[e]], axis=0)
                for e in range(2)
            ]
            even, odd = before_dot(0, y[0]), before_dot(2, y[1])
            for half, v in ((0, even + odd), (1, even - odd)):
                ks = pl.ds(k * n + half * h, h)
                for ref, ls in ((zs, slice(0, h)), (zd, slice(h, n))):
                    z = jnp.concatenate([v[:h, ls], v[h:, ls]], axis=1)
                    ref[ks, :n], ref[ks, n:] = split(z)
        p0[...] = after_dot(zs, 1)
        p1[...] = after_dot(zd, 3)
        for r0 in range(0, n, ch):
            rs = pl.ds(r0, ch)
            bs = pl.ds(r0 // 8, nb)
            ar, ai = win[0, rs, :], win[1, rs, :]
            o_re = jnp.zeros((ch, n), F32)
            o_im = jnp.zeros((ch, n), F32)
            for k in range(modes):
                ks = pl.ds(k * n + r0, ch)
                e, o = p0[ks, :], p1[ks, :]
                lhs, rhs = e + o, e - o
                br = jnp.concatenate([lhs[:, :h], rhs[:, :h]], axis=1)
                bi = jnp.concatenate([lhs[:, h:], rhs[:, h:]], axis=1)
                pr, pi = probe[k, 0, rs, :], probe[k, 1, rs, :]
                o_re = o_re + (pr * br + pi * bi)
                o_im = o_im + (pr * bi - pi * br)
                pg[bs, 2 * k] += (ar * br + ai * bi).reshape(nb, 8, n)
                pg[bs, 2 * k + 1] += (ar * bi - ai * br).reshape(nb, 8, n)

            for comp, v in ((0, o_re), (1, o_im)):
                add_shifted(tot, comp, v, r0, r8, rr, q, rem)

    lax.fori_loop(0, count[0], visit, 0)
    outs = [
        (tot.at[:, rows, cols], core_o),
        (tot.at[:, rows, lo], left_o),
        (tot.at[:, rows, hi], right_o),
    ]
    if early:
        outs += [(pg, pg_o)]
    else:
        half = n // 16
        give, keep = pl.ds((1 - bit[0]) * half, half), pl.ds(bit[0] * half, half)
        outs += [(pg.at[give], give_o), (pg.at[keep], keep_o)]
        outs += [(tot.at[:, top, :], up_o), (tot.at[:, bot, :], down_o)]
    stores = copies(outs, sems)
    for copy in stores:
        copy.start()
    for copy in stores:
        copy.wait()


def tile_grads(count, offs, bit, obj, halos, probe, amps):
    early = len(halos) == 2
    modes, _, n, _ = probe.shape
    h = n // 2
    _, tr, tc = obj.shape
    vmem = pl.BlockSpec(memory_space=pltpu.VMEM)
    smem = pl.BlockSpec(memory_space=pltpu.SMEM)
    anyw = pl.BlockSpec(memory_space=pl.ANY)
    shape = lambda *dims: jax.ShapeDtypeStruct(dims, F32)
    rows, cols = tr + n, tc + n
    blocks = n // 8
    outs = [shape(2, tr, tc), shape(2, tr, h), shape(2, tr, h)]
    if early:
        outs += [shape(blocks, 2 * modes + 1, 8, n)]
    else:
        outs += [shape(2, h, cols)] * 2 + [shape(blocks // 2, 2 * modes + 1, 8, n)] * 2
    return pl.pallas_call(
        functools.partial(grads_kernel, modes=modes, n=n, tr=tr, tc=tc, early=early),
        out_shape=tuple(outs),
        in_specs=[smem, smem, smem] + [anyw] * (1 + len(halos)) + [vmem] * 4,
        out_specs=[anyw] * len(outs),
        scratch_shapes=[
            pltpu.VMEM((2, rows, cols), F32),
            pltpu.VMEM((2, rows, cols), F32),
            pltpu.VMEM((n // 8, 2 * modes + 1, 8, n), F32),
            pltpu.VMEM((2, n, n), F32),
            pltpu.VMEM((modes * n, 2 * n), BF16),
            pltpu.VMEM((modes * n, 2 * n), BF16),
            pltpu.VMEM((modes * n, n), F32),
            pltpu.VMEM((modes * n, n), F32),
            pltpu.VMEM((modes, 2, n, n), F32),
            pltpu.VMEM((2, n, h), F32),
            pltpu.SemaphoreType.DMA((10,)),
        ],
        compiler_params=pltpu.CompilerParams(vmem_limit_bytes=56 * MIB),
        cost_estimate=pl.CostEstimate(flops=40_000_000_000, bytes_accessed=30_000_000, transcendentals=0),
        name="tile_grads_early" if early else "tile_grads_late",
    )(count, offs, bit, obj, *halos, probe, amps, *tables(n))


def object_update(obj, core, illum, left, right, above, below):
    _, tr, tc = obj.shape
    h = left.shape[-1]
    total = core + jnp.pad(left, ((0, 0), (0, 0), (0, tc - h)))
    total = total + jnp.pad(right, ((0, 0), (0, 0), (tc - h, 0)))
    total = total + jnp.pad(above[:, :, h : h + tc], ((0, 0), (0, tr - h), (0, 0)))
    total = total + jnp.pad(below[:, :, h : h + tc], ((0, 0), (tr - h, 0), (0, 0)))
    return obj - total / illum


def moved(block, axis, distance):
    count = lax.axis_size(axis)
    route = [(i, i + distance) for i in range(count) if 0 <= i + distance < count]
    return lax.ppermute(block, axis, route)


def place(flat):
    w, n = flat // 8, flat % 8
    return {"core": w % 2, "x": w // 4, "y": (n // 4) * 2 + (w // 2) % 2, "z": n % 4}


def flat_of(at):
    w = at["x"] * 4 + (at["y"] % 2) * 2 + at["core"]
    n = (at["y"] // 2) * 4 + at["z"]
    return w * 8 + n


def route(axes, hop):
    pairs = []
    for i in range(128):
        at = place(i)
        axis = axes[at["core"]]
        at[axis] = (at[axis] + hop) % (2 if axis == "core" else 4)
        pairs.append((i, flat_of(at)))
    return pairs


def around(piece, axes):
    return [lax.ppermute(piece, BOTH, route(axes, hop)) for hop in (1, 2, 3)]


def own_core():
    return lax.axis_index("wide") & 1


def probe_update(give, keep, probe, arrived):
    w, n = lax.axis_index("wide"), lax.axis_index("narrow")
    core, x, z = w & 1, w >> 2, n & 3
    cut = give.shape[0] // 4
    got = [
        lax.ppermute(give[i * cut : (i + 1) * cut], BOTH, route(("core", "core"), 1))
        for i in range(4)
    ]
    v = keep + jnp.concatenate(got, axis=0)

    def scattered(v, t, axis):
        size = v.shape[0] // 4
        part = lambda d: lax.dynamic_slice_in_dim(v, (d & 3) * size, size, 0)
        got = [
            lax.ppermute(part(t + hop), BOTH, route((axis, axis), hop)) for hop in (1, 2, 3)
        ]
        return part(t) + got[0] + got[1] + got[2]

    v = scattered(v, x, "x")
    v, arrived = lax.optimization_barrier((v, arrived))
    v = scattered(v, z, "z")
    a, b, c = around(v, ("y", "y"))
    v = (v + a + b + c)[0]
    modes, _, size, _ = probe.shape
    block = core * 16 + x * 4 + z
    mine = lax.dynamic_slice_in_dim(probe.reshape(2 * modes, size, size), block * 8, 8, 1)
    mine = mine - v[: 2 * modes] / (v[2 * modes] + step_floor)

    def gathered(piece, t, axes):
        pieces = [piece, *around(piece, axes)]
        rows = []
        for d in range(4):
            j = (t - d) & 3
            one = jnp.where(j < 2, jnp.where(j == 0, *pieces[:2]), jnp.where(j == 2, *pieces[2:]))
            rows.append(one)
        return jnp.concatenate(rows, axis=1)

    return mine, arrived, gathered


def probe_gather(mine, gathered, sides, update):
    w, n = lax.axis_index("wide"), lax.axis_index("narrow")
    core, x, z = w & 1, w >> 2, n & 3
    mine = gathered(mine, jnp.where(core == 0, z, x), ("z", "x"))
    mine, sides = lax.optimization_barrier((mine, sides))
    new_object = update(*sides)
    mine = gathered(mine, jnp.where(core == 0, x, z), ("x", "z"))
    mine, new_object = lax.optimization_barrier((mine, new_object))
    got = lax.ppermute(mine, BOTH, route(("core", "core"), 1))
    first = jnp.where(core == 0, mine, got)
    second = jnp.where(core == 0, got, mine)
    planes, _, size = mine.shape
    second = second.reshape(planes, 4, 4, 8, size).swapaxes(1, 2).reshape(first.shape)
    return jnp.concatenate([first, second], axis=1), new_object


def on_device(object_field, probe_modes, amplitudes, offsets, counts):
    h = probe_modes.shape[-1] // 2
    _, tr, tc = object_field.shape
    count, offs, bit = counts[0], offsets[:, 0, 0], own_core()[None]
    mine = jnp.concatenate([count, offs[0], offs[1]]).astype(F32)
    mine = jnp.broadcast_to(jnp.pad(mine, (0, h - mine.shape[0])), (2, 8, h))
    up = moved(object_field[:, tr - h :], "narrow", 1)
    down = moved(object_field[:, :h], "narrow", -1)
    tagged = lambda cols: jnp.concatenate([object_field[:, :, cols], mine], axis=1)
    left = moved(tagged(slice(tc - h, tc)), "wide", 1)
    right = moved(tagged(slice(0, h)), "wide", -1)
    tags = jnp.stack([left[:1, tr:], right[:1, tr:]])
    corner = lambda rows: jnp.concatenate(
        [
            jnp.stack([left[:, rows], right[:, rows]]),
            jnp.concatenate([tags, jnp.stack([mine[:1]] * 2)], axis=1),
        ],
        axis=2,
    )
    eup = moved(corner(slice(tr - h, tr)), "narrow", 1)
    edown = moved(corner(slice(0, h)), "narrow", -1)
    core_e, left_e, right_e, pg_e = tile_grads(
        count, offs, bit, object_field, (left, right), probe_modes, amplitudes[0, 0]
    )
    row = lambda e: [e[0, 0, h, :16], e[0, 1, h, :16], e[1, 0, h, :16]]
    info = row(eup) + [left[0, tr, :16], mine[0, 0, :16], right[0, tr, :16]] + row(edown)
    info = jnp.stack(info).astype(jnp.int32)
    illum = tile_illum(info, probe_modes, tr, tc, offs.shape[-1])
    core, left_g, right_g, up_g, down_g, give, keep = tile_grads(
        count, offs, bit, object_field, (left, right, up, down, eup, edown, pg_e),
        probe_modes, amplitudes[0, 0],
    )
    below = moved(up_g, "narrow", -1)
    above = moved(down_g, "narrow", 1)
    arrived = (above, below, illum)
    block, (above, below, illum), gathered = probe_update(give, keep, probe_modes, arrived)
    side = lambda strip, cols: (
        strip
        + jnp.pad(above[:, :, cols], ((0, 0), (0, tr - h), (0, 0)))
        + jnp.pad(below[:, :, cols], ((0, 0), (tr - h, 0), (0, 0)))
    )
    sides = (
        side(left_e + left_g, slice(0, h)),
        side(right_e + right_g, slice(h + tc, 2 * h + tc)),
    )
    block, sides = lax.optimization_barrier((block, sides))
    from_right = moved(sides[0], "wide", -1)
    from_left = moved(sides[1], "wide", 1)
    update = lambda a, b: object_update(object_field, core_e + core, illum, a, b, above, below)
    new_probe, new_object = probe_gather(block, gathered, (from_left, from_right), update)
    return (new_object, new_probe.reshape(probe_modes.shape))


def solution(mesh):
    return jax.shard_map(
        on_device,
        mesh=mesh,
        in_specs=(
            P(None, "narrow", "wide"),
            P(),
            P("narrow", "wide", None, None, None),
            P(None, "narrow", "wide", None),
            P("narrow", "wide"),
        ),
        out_specs=(P(None, "narrow", "wide"), P()),
        check_vma=False,
    )
```

```python
import functools

import jax
import jax.numpy as jnp
import numpy as np
from jax import lax
from jax.experimental import pallas as pl
from jax.experimental.pallas import tpu as pltpu
from jax.sharding import PartitionSpec as P

amp_floor = 0.25
step_floor = 1.0
F32 = jnp.float32
BF16 = jnp.bfloat16
BOTH = ("wide", "narrow")
MIB = 1024 * 1024


def tables(length):
    half = length // 2
    row = np.arange(half)[:, None]
    col = np.arange(half)[None, :]
    pairs = []
    for odd in (0, 1):
        angle = -2.0 * np.pi * (row * (2 * col + odd) % length) / length
        re = np.cos(angle) / np.sqrt(length)
        im = np.sin(angle) / np.sqrt(length)
        matrix = np.block([[re, im], [-im, re]]).astype(np.float32)
        for table in (matrix, matrix.T):
            high = table.astype(jnp.bfloat16)
            low = (table - high.astype(np.float32)).astype(jnp.bfloat16)
            pairs.append((high, low))
    both = np.stack([np.stack(pair) for pair in pairs])
    order = np.zeros((length, length), np.float32)
    for k in range(half):
        order[2 * k, k] = 1
        order[2 * k + 1, half + k] = 1
    order = np.concatenate([order, order], 0).astype(jnp.bfloat16)
    return jnp.asarray(both), jnp.asarray(order)


def split(x):
    high = x.astype(BF16)
    return high, (x - high.astype(F32)).astype(BF16)


def dot(a, b):
    return jnp.dot(a, b, preferred_element_type=F32)


def add_shifted(tot, comp, v, r0, r8, rr, q, rem):
    ch, n = v.shape
    h, nb = n // 2, ch // 8
    fwd_lanes = jnp.where(rem == h, 0, rem)
    fwd_rows = jnp.where(rr == 8, 0, rr)
    past = lax.broadcasted_iota(jnp.int32, (ch + 8, h), 1) >= rem
    below = lax.broadcasted_iota(jnp.int32, (nb + 1, 8, h), 1) >= rr

    def lowered(v):
        g = pltpu.roll(v.reshape(nb, 8, h), fwd_rows, axis=1)
        zero = jnp.zeros((1, 8, h), F32)
        here = jnp.concatenate([g, zero], axis=0)
        above = jnp.concatenate([zero, g], axis=0)
        return pltpu.roll(jnp.where(below, here, above).reshape(ch + 8, h), fwd_lanes, axis=1)

    t0, t1 = lowered(v[:, :h]), lowered(v[:, h:])
    zero = jnp.zeros_like(t0)
    full = [jnp.where(past, t0, zero), jnp.where(past, t1, t0), jnp.where(past, zero, t1)]
    tot[comp, pl.ds(r8 + r0, ch + 8), pl.ds(q, 3 * h)] += jnp.concatenate(full, axis=1)


def window_place(offs, s, rows, cols, n):
    h = n // 2
    r, c = offs[0, s], offs[1, s]
    q = jnp.minimum(c // h, (cols - 3 * h) // h)
    rem = c - q * h
    r8 = jnp.minimum(r // 8, (rows - n - 8) // 8)
    rr = r - r8 * 8
    return pl.multiple_of(r8 * 8, 8), rr, pl.multiple_of(q * h, h), rem


def copies(pairs, sems):
    return [pltpu.make_async_copy(a, b, sems.at[i]) for i, (a, b) in enumerate(pairs)]


def illum_kernel(info, probe, out, tot, one, *, modes, n, tr, tc, slots):
    h, ch = n // 2, 64
    tot[...] = jnp.zeros_like(tot)
    for r0 in range(0, n, ch):
        rs = pl.ds(r0, ch)
        acc = jnp.zeros((ch, n), F32)
        for k in range(modes):
            for c in range(2):
                v = probe[k, c, rs, :]
                acc = acc + v * v
        one[rs, :] = acc

    def visit(i, carry):
        t, s = i // slots, i % slots
        live = s < info[t, 0]
        r = jnp.where(live, info[t, 1 + s], 0) + (t // 3 - 1) * tr + h
        c = jnp.where(live, info[t, 1 + slots + s], 0) + (t % 3 - 1) * tc + h

        @pl.when(live & (r > 0) & (r < tr + n) & (c > 0) & (c < tc + n))
        def _():
            r8 = pl.multiple_of(r // 8 * 8, 8)
            q = pl.multiple_of(c // h * h, h)
            for r0 in range(0, n, ch):
                add_shifted(tot, 0, one[pl.ds(r0, ch), :], r0, r8, r - r8, q, c - q)

        return carry

    lax.fori_loop(0, 9 * slots, visit, 0)
    out[...] = tot[0, n : n + tr, n : n + tc] + step_floor


def tile_illum(info, probe, tr, tc, slots):
    modes, _, n, _ = probe.shape
    vmem = pl.BlockSpec(memory_space=pltpu.VMEM)
    smem = pl.BlockSpec(memory_space=pltpu.SMEM)
    return pl.pallas_call(
        functools.partial(illum_kernel, modes=modes, n=n, tr=tr, tc=tc, slots=slots),
        out_shape=jax.ShapeDtypeStruct((tr, tc), F32),
        in_specs=[smem, vmem],
        out_specs=vmem,
        scratch_shapes=[pltpu.VMEM((1, tr + 2 * n, tc + 2 * n), F32), pltpu.VMEM((n, n), F32)],
        compiler_params=pltpu.CompilerParams(vmem_limit_bytes=16 * MIB),
        cost_estimate=pl.CostEstimate(flops=0, bytes_accessed=0, transcendentals=0),
        name="tile_illum",
    )(info, probe)


def grads_kernel(*refs, modes, n, tr, tc, early):
    count, offs, bit, obj, left, right, *refs = refs
    if early:
        probe, amps, table, order, core_o, left_o, right_o, pg_o, *refs = refs
    else:
        up, down, eup, edown, pg_e, probe, amps, table, order, *refs = refs
        core_o, left_o, right_o, up_o, down_o, give_o, keep_o, *refs = refs
    ext, tot, pg, win, zs, zd, p0, p1, u, ap, sems = refs
    h = n // 2
    ch = 64
    nb = ch // 8
    rows, cols = pl.ds(h, tr), pl.ds(h, tc)
    lo, hi = pl.ds(0, h), pl.ds(h + tc, h)
    top, bot = pl.ds(0, h), pl.ds(h + tr, h)
    places_in = [
        (obj, ext.at[:, rows, cols]),
        (left.at[:, pl.ds(0, tr), :], ext.at[:, rows, lo]),
        (right.at[:, pl.ds(0, tr), :], ext.at[:, rows, hi]),
    ]
    if not early:
        places_in += [
            (up, ext.at[:, top, cols]),
            (down, ext.at[:, bot, cols]),
            (eup.at[0, :, lo, :], ext.at[:, top, lo]),
            (eup.at[1, :, lo, :], ext.at[:, top, hi]),
            (edown.at[0, :, lo, :], ext.at[:, bot, lo]),
            (edown.at[1, :, lo, :], ext.at[:, bot, hi]),
            (pg_e, pg),
        ]
    loads = copies(places_in, sems)
    for copy in loads:
        copy.start()
    tot[...] = jnp.zeros_like(tot)
    if early:
        pg[...] = jnp.zeros_like(pg)
    for copy in loads:
        copy.wait()

    lane = lax.broadcasted_iota(jnp.int32, (ch + 8, h), 1)
    sub = lax.broadcasted_iota(jnp.int32, (nb, 8, h), 1)

    def after_dot(z, i):
        high, low = table[i, 0], table[i, 1]
        return dot(z[:, :n], high) + (dot(z[:, n:], high) + dot(z[:, :n], low))

    def before_dot(i, y):
        high, low = split(y)
        return dot(table[i, 0], high) + (dot(table[i, 0], low) + dot(table[i, 1], high))

    def visit(s, carry):
        inside = (offs[0, s] >= h) & (offs[0, s] <= tr + h - n)
        pl.when(inside if early else ~inside)(lambda: slot(s))
        return carry

    def slot(s):
        r8, rr, q, rem = window_place(offs, s, tr + n, tc + n, n)
        back_lanes = jnp.where((rem == 0) | (rem == h), 0, h - rem)
        back_rows = jnp.where((rr == 0) | (rr == 8), 0, 8 - rr)
        for r0 in range(0, n, ch):
            rs = pl.ds(r0, ch)
            w = []
            for comp in range(2):
                blk = ext[comp, pl.ds(r8 + r0, ch + 8), pl.ds(q, 3 * h)]
                t = [pltpu.roll(blk[:, j * h : (j + 1) * h], back_lanes, axis=1) for j in range(3)]
                keep = lane < h - rem
                sides = []
                for x, y in ((t[0], t[1]), (t[1], t[2])):
                    g = jnp.where(keep, x, y).reshape(nb + 1, 8, h)
                    g = pltpu.roll(g, back_rows, axis=1)
                    sides.append(jnp.where(sub < 8 - rr, g[:-1], g[1:]).reshape(ch, h))
                v = jnp.concatenate(sides, axis=1)
                win[comp, rs, :] = v
                w.append(v)
            pg[pl.ds(r0 // 8, nb), 2 * modes] += (w[0] * w[0] + w[1] * w[1]).reshape(nb, 8, n)
        for k in range(modes):
            for r0 in range(0, n, ch):
                rs = pl.ds(r0, ch)
                ks = pl.ds(k * n + r0, ch)
                ar, ai = win[0, rs, :], win[1, rs, :]
                pr, pi = probe[k, 0, rs, :], probe[k, 1, rs, :]
                wr = pr * ar - pi * ai
                wi = pr * ai + pi * ar
                z = jnp.concatenate([wr[:, :h] + wr[:, h:], wi[:, :h] + wi[:, h:]], axis=1)
                zs[ks, :n], zs[ks, n:] = split(z)
                z = jnp.concatenate([wr[:, :h] - wr[:, h:], wi[:, :h] - wi[:, h:]], axis=1)
                zd[ks, :n], zd[ks, n:] = split(z)
        p0[...] = after_dot(zs, 0)
        p1[...] = after_dot(zd, 2)
        for k in range(modes):
            top, bot = pl.ds(k * n, h), pl.ds(k * n + h, h)

            def folded(sign):
                parts = []
                for ls in (slice(0, h), slice(h, n)):
                    parts.append(
                        jnp.concatenate([p[top, ls] + sign * p[bot, ls] for p in (p0, p1)], axis=1)
                    )
                return jnp.concatenate(parts, axis=0)

            u[k, 0] = before_dot(1, folded(1.0))
            u[k, 1] = before_dot(3, folded(-1.0))
        am = dot(jnp.concatenate(split(amps[s]), axis=1), order[...])
        ap[0] = am[:, :h]
        ap[1] = am[:, h:]
        factor = []
        for e in range(2):
            power = jnp.zeros((h, n), F32)
            for k in range(modes):
                a, b = u[k, e, :h, :], u[k, e, h:, :]
                power = power + (a * a + b * b)
            am = jnp.concatenate([ap[j, pl.ds(e, h, stride=2), :] for j in range(2)], axis=1)
            factor.append(1.0 - am * lax.rsqrt(power + amp_floor))
        for k in range(modes):
            y = [
                jnp.concatenate([u[k, e, :h, :] * factor[e], u[k, e, h:, :] * factor[e]], axis=0)
                for e in range(2)
            ]
            even, odd = before_dot(0, y[0]), before_dot(2, y[1])
            for half, v in ((0, even + odd), (1, even - odd)):
                ks = pl.ds(k * n + half * h, h)
                for ref, ls in ((zs, slice(0, h)), (zd, slice(h, n))):
                    z = jnp.concatenate([v[:h, ls], v[h:, ls]], axis=1)
                    ref[ks, :n], ref[ks, n:] = split(z)
        p0[...] = after_dot(zs, 1)
        p1[...] = after_dot(zd, 3)
        for r0 in range(0, n, ch):
            rs = pl.ds(r0, ch)
            bs = pl.ds(r0 // 8, nb)
            ar, ai = win[0, rs, :], win[1, rs, :]
            o_re = jnp.zeros((ch, n), F32)
            o_im = jnp.zeros((ch, n), F32)
            for k in range(modes):
                ks = pl.ds(k * n + r0, ch)
                e, o = p0[ks, :], p1[ks, :]
                lhs, rhs = e + o, e - o
                br = jnp.concatenate([lhs[:, :h], rhs[:, :h]], axis=1)
                bi = jnp.concatenate([lhs[:, h:], rhs[:, h:]], axis=1)
                pr, pi = probe[k, 0, rs, :], probe[k, 1, rs, :]
                o_re = o_re + (pr * br + pi * bi)
                o_im = o_im + (pr * bi - pi * br)
                pg[bs, 2 * k] += (ar * br + ai * bi).reshape(nb, 8, n)
                pg[bs, 2 * k + 1] += (ar * bi - ai * br).reshape(nb, 8, n)

            for comp, v in ((0, o_re), (1, o_im)):
                add_shifted(tot, comp, v, r0, r8, rr, q, rem)

    lax.fori_loop(0, count[0], visit, 0)
    outs = [
        (tot.at[:, rows, cols], core_o),
        (tot.at[:, rows, lo], left_o),
        (tot.at[:, rows, hi], right_o),
    ]
    if early:
        outs += [(pg, pg_o)]
    else:
        half = n // 16
        give, keep = pl.ds((1 - bit[0]) * half, half), pl.ds(bit[0] * half, half)
        outs += [(pg.at[give], give_o), (pg.at[keep], keep_o)]
        outs += [(tot.at[:, top, :], up_o), (tot.at[:, bot, :], down_o)]
    stores = copies(outs, sems)
    for copy in stores:
        copy.start()
    for copy in stores:
        copy.wait()


def tile_grads(count, offs, bit, obj, halos, probe, amps):
    early = len(halos) == 2
    modes, _, n, _ = probe.shape
    h = n // 2
    _, tr, tc = obj.shape
    vmem = pl.BlockSpec(memory_space=pltpu.VMEM)
    smem = pl.BlockSpec(memory_space=pltpu.SMEM)
    anyw = pl.BlockSpec(memory_space=pl.ANY)
    shape = lambda *dims: jax.ShapeDtypeStruct(dims, F32)
    rows, cols = tr + n, tc + n
    blocks = n // 8
    outs = [shape(2, tr, tc), shape(2, tr, h), shape(2, tr, h)]
    if early:
        outs += [shape(blocks, 2 * modes + 1, 8, n)]
    else:
        outs += [shape(2, h, cols)] * 2 + [shape(blocks // 2, 2 * modes + 1, 8, n)] * 2
    return pl.pallas_call(
        functools.partial(grads_kernel, modes=modes, n=n, tr=tr, tc=tc, early=early),
        out_shape=tuple(outs),
        in_specs=[smem, smem, smem] + [anyw] * (1 + len(halos)) + [vmem] * 4,
        out_specs=[anyw] * len(outs),
        scratch_shapes=[
            pltpu.VMEM((2, rows, cols), F32),
            pltpu.VMEM((2, rows, cols), F32),
            pltpu.VMEM((n // 8, 2 * modes + 1, 8, n), F32),
            pltpu.VMEM((2, n, n), F32),
            pltpu.VMEM((modes * n, 2 * n), BF16),
            pltpu.VMEM((modes * n, 2 * n), BF16),
            pltpu.VMEM((modes * n, n), F32),
            pltpu.VMEM((modes * n, n), F32),
            pltpu.VMEM((modes, 2, n, n), F32),
            pltpu.VMEM((2, n, h), F32),
            pltpu.SemaphoreType.DMA((10,)),
        ],
        compiler_params=pltpu.CompilerParams(vmem_limit_bytes=34 * MIB),
        cost_estimate=pl.CostEstimate(flops=40_000_000_000, bytes_accessed=30_000_000, transcendentals=0),
        name="tile_grads_early" if early else "tile_grads_late",
    )(count, offs, bit, obj, *halos, probe, amps, *tables(n))


def update_kernel(obj, core_e, core, illum, left, right, above, below, out):
    step, h, tc = pl.program_id(0), left.shape[-1], obj.shape[-1]
    out[...] = core_e[...] + core[...]

    @pl.when(step == 0)
    def _():
        out[...] += above[:, :, h : h + tc]

    @pl.when(step == pl.num_programs(0) - 1)
    def _():
        out[...] += below[:, :, h : h + tc]

    out[:, :, :h] += left[...]
    out[:, :, tc - h :] += right[...]
    out[...] = obj[...] - out[...] / illum[...]


def object_update(obj, core_e, core, illum, left, right, above, below):
    _, tr, tc = obj.shape
    h = left.shape[-1]
    tile = pl.BlockSpec((2, h, tc), lambda i: (0, i, 0))
    side = pl.BlockSpec((2, h, h), lambda i: (0, i, 0))
    strip = pl.BlockSpec((2, h, above.shape[-1]), lambda i: (0, 0, 0))
    return pl.pallas_call(
        update_kernel,
        grid=(tr // h,),
        out_shape=jax.ShapeDtypeStruct(obj.shape, F32),
        in_specs=[tile, tile, tile, pl.BlockSpec((h, tc), lambda i: (i, 0)), side, side, strip, strip],
        out_specs=tile,
        compiler_params=pltpu.CompilerParams(vmem_limit_bytes=56 * MIB),
        cost_estimate=pl.CostEstimate(flops=10_000_000, bytes_accessed=20_000_000, transcendentals=0),
        name="object_update",
    )(obj, core_e, core, illum, left, right, above, below)


def moved(block, axis, distance):
    count = lax.axis_size(axis)
    route = [(i, i + distance) for i in range(count) if 0 <= i + distance < count]
    return lax.ppermute(block, axis, route)


def place(flat):
    w, n = flat // 8, flat % 8
    return {"core": w % 2, "x": w // 4, "y": (n // 4) * 2 + (w // 2) % 2, "z": n % 4}


def flat_of(at):
    w = at["x"] * 4 + (at["y"] % 2) * 2 + at["core"]
    n = (at["y"] // 2) * 4 + at["z"]
    return w * 8 + n


def route(axes, hop):
    pairs = []
    for i in range(128):
        at = place(i)
        axis = axes[at["core"]]
        at[axis] = (at[axis] + hop) % (2 if axis == "core" else 4)
        pairs.append((i, flat_of(at)))
    return pairs


def around(piece, axes):
    return [lax.ppermute(piece, BOTH, route(axes, hop)) for hop in (1, 2, 3)]


def own_core():
    return lax.axis_index("wide") & 1


def probe_update(give, keep, probe, arrived):
    w, n = lax.axis_index("wide"), lax.axis_index("narrow")
    core, x, z = w & 1, w >> 2, n & 3
    cut = give.shape[0] // 4
    got = [
        lax.ppermute(give[i * cut : (i + 1) * cut], BOTH, route(("core", "core"), 1))
        for i in range(4)
    ]
    v = keep + jnp.concatenate(got, axis=0)

    def scattered(v, t, axis):
        size = v.shape[0] // 4
        part = lambda d: lax.dynamic_slice_in_dim(v, (d & 3) * size, size, 0)
        got = [
            lax.ppermute(part(t + hop), BOTH, route((axis, axis), hop)) for hop in (1, 2, 3)
        ]
        return part(t) + got[0] + got[1] + got[2]

    v = scattered(v, x, "x")
    v = scattered(v, z, "z")
    v, arrived = lax.optimization_barrier((v, arrived))
    a, b, c = around(v, ("y", "y"))
    v = (v + a + b + c)[0]
    modes, _, size, _ = probe.shape
    block = core * 16 + x * 4 + z
    mine = lax.dynamic_slice_in_dim(probe.reshape(2 * modes, size, size), block * 8, 8, 1)
    mine = mine - v[: 2 * modes] / (v[2 * modes] + step_floor)

    def gathered(piece, t, axes):
        pieces = [piece, *around(piece, axes)]
        rows = []
        for d in range(4):
            j = (t - d) & 3
            one = jnp.where(j < 2, jnp.where(j == 0, *pieces[:2]), jnp.where(j == 2, *pieces[2:]))
            rows.append(one)
        return jnp.concatenate(rows, axis=1)

    return mine, arrived, gathered


def probe_gather(mine, gathered, sides, update):
    w, n = lax.axis_index("wide"), lax.axis_index("narrow")
    core, x, z = w & 1, w >> 2, n & 3
    mine = gathered(mine, jnp.where(core == 0, z, x), ("z", "x"))
    mine, sides = lax.optimization_barrier((mine, sides))
    new_object = update(*sides)
    mine = gathered(mine, jnp.where(core == 0, x, z), ("x", "z"))
    mine, new_object = lax.optimization_barrier((mine, new_object))
    got = lax.ppermute(mine, BOTH, route(("core", "core"), 1))
    first = jnp.where(core == 0, mine, got)
    second = jnp.where(core == 0, got, mine)
    planes, _, size = mine.shape
    second = second.reshape(planes, 4, 4, 8, size).swapaxes(1, 2).reshape(first.shape)
    return jnp.concatenate([first, second], axis=1), new_object


def on_device(object_field, probe_modes, amplitudes, offsets, counts):
    h = probe_modes.shape[-1] // 2
    _, tr, tc = object_field.shape
    count, offs, bit = counts[0], offsets[:, 0, 0], own_core()[None]
    mine = jnp.concatenate([count, offs[0], offs[1]]).astype(F32)
    mine = jnp.broadcast_to(jnp.pad(mine, (0, h - mine.shape[0])), (2, 8, h))
    up = moved(object_field[:, tr - h :], "narrow", 1)
    down = moved(object_field[:, :h], "narrow", -1)
    tagged = lambda cols: jnp.concatenate([object_field[:, :, cols], mine], axis=1)
    left = moved(tagged(slice(tc - h, tc)), "wide", 1)
    right = moved(tagged(slice(0, h)), "wide", -1)
    tags = jnp.stack([left[:1, tr:], right[:1, tr:]])
    corner = lambda rows: jnp.concatenate(
        [
            jnp.stack([left[:, rows], right[:, rows]]),
            jnp.concatenate([tags, jnp.stack([mine[:1]] * 2)], axis=1),
        ],
        axis=2,
    )
    eup = moved(corner(slice(tr - h, tr)), "narrow", 1)
    edown = moved(corner(slice(0, h)), "narrow", -1)
    core_e, left_e, right_e, pg_e = tile_grads(
        count, offs, bit, object_field, (left, right), probe_modes, amplitudes[0, 0]
    )
    row = lambda e: [e[0, 0, h, :16], e[0, 1, h, :16], e[1, 0, h, :16]]
    info = row(eup) + [left[0, tr, :16], mine[0, 0, :16], right[0, tr, :16]] + row(edown)
    info = jnp.stack(info).astype(jnp.int32)
    illum = tile_illum(info, probe_modes, tr, tc, offs.shape[-1])
    core, left_g, right_g, up_g, down_g, give, keep = tile_grads(
        count, offs, bit, object_field, (left, right, up, down, eup, edown, pg_e),
        probe_modes, amplitudes[0, 0],
    )
    below = moved(up_g, "narrow", -1)
    above = moved(down_g, "narrow", 1)
    arrived = (above, below, illum)
    block, (above, below, illum), gathered = probe_update(give, keep, probe_modes, arrived)
    side = lambda strip, cols: (
        strip
        + jnp.pad(above[:, :, cols], ((0, 0), (0, tr - h), (0, 0)))
        + jnp.pad(below[:, :, cols], ((0, 0), (tr - h, 0), (0, 0)))
    )
    sides = (
        side(left_e + left_g, slice(0, h)),
        side(right_e + right_g, slice(h + tc, 2 * h + tc)),
    )
    block, sides = lax.optimization_barrier((block, sides))
    from_right = moved(sides[0], "wide", -1)
    from_left = moved(sides[1], "wide", 1)
    update = lambda a, b: object_update(
        object_field, core_e, core, illum, a, b, above, below
    )
    new_probe, new_object = probe_gather(block, gathered, (from_left, from_right), update)
    return (new_object, new_probe.reshape(probe_modes.shape))


def solution(mesh):
    return jax.shard_map(
        on_device,
        mesh=mesh,
        in_specs=(
            P(None, "narrow", "wide"),
            P(),
            P("narrow", "wide", None, None, None),
            P(None, "narrow", "wide", None),
            P("narrow", "wide"),
        ),
        out_specs=(P(None, "narrow", "wide"), P()),
        check_vma=False,
    )
```
